128 devices in a mesh: dp: 8 (over y_lo, x), seq: 8 (over z, core), branch: 2 (over y_hi).
Axes of the slice: x: 4, y: 4 (y_hi: 2, y_lo: 2; y = y_hi * 2 + y_lo), z: 4, core: 2. Of those that a mesh axis runs over, the one named last changes fastest.
Arguments:
- inputs: bfloat16 [8, 2048, 2048], P('dp', ('seq', 'branch')), may hold values from -6 to 6
- segment_ids: int32 [8, 2048], P('dp'), may hold values from 0 to 4, as said below
- valid_mask: int32 [8, 2048], P('dp'), may hold values from 0 to 1, as said below
- norm_gain: bfloat16 [2048], replicated, may hold values from 0.5 to 1.5
- norm_bias: bfloat16 [2048], replicated, may hold values from -2 to 2
- qkv_weight: bfloat16 [2048, 3, 2048], P(('dp', 'seq'), None, 'branch'), may hold values from -0.125 to 0.125
- qkv_bias: bfloat16 [3, 2048], P(None, 'branch'), may hold values from -3 to 3
- attn_out_weight: bfloat16 [2048, 2048], P(('dp', 'seq'), 'branch'), may hold values from -0.75 to 0.75
- up_weight: bfloat16 [2048, 8192], P(('dp', 'seq'), 'branch'), may hold values from -0.125 to 0.125
- up_bias: bfloat16 [8192], P('branch'), may hold values from -3 to 3
- down_weight: bfloat16 [2048, 8192], P(('dp', 'seq'), 'branch'), may hold values from -0.0625 to 0.0625
- out_bias: bfloat16 [2048], replicated, may hold values from -3 to 3
- grad_out: bfloat16 [8, 2048, 2048], P('dp', ('seq', 'branch')), may hold values from -6 to 6
Outputs:
- output: bfloat16 [8, 2048, 2048], P('dp', ('seq', 'branch'))
- grad_inputs: float32 [8, 2048, 2048], P('dp', ('seq', 'branch'))
- grad_norm_gain: float32 [2048], replicated
- grad_norm_bias: float32 [2048], replicated
- grad_qkv_weight: float32 [2048, 3, 2048], P(('dp', 'seq'), None, 'branch')
- grad_qkv_bias: float32 [3, 2048], P(None, 'branch')
- grad_attn_out_weight: float32 [2048, 2048], P(('dp', 'seq'), 'branch')
- grad_up_weight: float32 [2048, 8192], P(('dp', 'seq'), 'branch')
- grad_up_bias: float32 [8192], P('branch')
- grad_down_weight: float32 [2048, 8192], P(('dp', 'seq'), 'branch')
- grad_out_bias: float32 [2048], replicated
The draws below stay inside these ranges and needn't reach their ends.
Inputs may be any that keep to these rules, and one draw needn't show every extreme that they name: `segment_ids`: within a row the ids never fall and each of the documents 0 to 4 is present; padding tokens carry the id of the last document. `valid_mask`: 0 exactly on a run of padding of two tokens or more at the end of each row.
All inputs are finite; a program needn't handle non-finite values.
Results may differ from the reference program's by a relative error of at most 0.013.
Values may be sent and summed in bfloat16 or wider, within the bound.
A program may use at most 256 MiB of HBM per device.

```python
import jax
import jax.numpy as jnp
from jax import lax

D = 2048
H = 32
HD = 64
ROT = 32
FF = 8192
LEN = 2048
ROWS = 8
N_SEQ = 8


def row_cuts(key):
    shard = LEN // N_SEQ
    parts = jax.random.split(key, 5)
    long_start = jax.random.randint(parts[0], (ROWS,), shard // 4, shard // 2)
    first_cut = jax.random.randint(parts[1], (ROWS,), 1, long_start)
    long_end = LEN - shard + jax.random.randint(parts[2], (ROWS,), shard // 4, shard // 2)
    padding = jax.random.randint(parts[3], (ROWS,), 2, shard // 4 + 2)
    pad_start = LEN - padding
    last_cut = jax.random.randint(parts[4], (ROWS,), long_end + 1, pad_start)
    return (first_cut, long_start, long_end, last_cut, pad_start)


def draw_segment_ids(key, part):
    first_cut, long_start, long_end, last_cut, pad_start = row_cuts(key)
    place = jnp.arange(LEN, dtype=jnp.int32)[None, :]
    result = (place >= first_cut[:, None]).astype(jnp.int32)
    result = result + (place >= long_start[:, None]).astype(jnp.int32)
    result = result + (place >= long_end[:, None]).astype(jnp.int32)
    result = result + (place >= last_cut[:, None]).astype(jnp.int32)
    return result


def draw_valid_mask(key, part):
    first_cut, long_start, long_end, last_cut, pad_start = row_cuts(key)
    place = jnp.arange(LEN, dtype=jnp.int32)[None, :]
    return (place < pad_start[:, None]).astype(jnp.int32)


def level_of(rng, dims, pieces, low, top_value):
    def one(position, blocks):
        draws = jax.random.uniform(jax.random.fold_in(jax.random.fold_in(rng, 6), position), (blocks,), jnp.float32, low / len(pieces), top_value / len(pieces))
        return jnp.repeat(jnp.exp(draws), dims[position] // blocks).reshape((-1,) + (1,) * (len(dims) - position - 1))

    factor_of = one(*pieces[0])
    for cut in pieces[1:]:
        factor_of = factor_of * one(*cut)
    return factor_of


def bell_draw(rng, dims, width, limit, cuts=(), kind=jnp.bfloat16):
    level = level_of(rng, dims, cuts, -0.22, 0.18) if cuts else 1.0
    values = jax.random.normal(rng, dims, jnp.float32) * width * level
    return jnp.minimum(jnp.maximum(values, -limit), limit).astype(kind)


def setup_inputs(seed: int = 0) -> dict:
    streams_of = jax.random.split(jax.random.key(seed), 14)
    inputs = bell_draw(streams_of[0], (ROWS, LEN, D), 1.0, 6.0, ((0, 8), (1, 16)))
    segment_ids = draw_segment_ids(jax.random.fold_in(streams_of[13], 71), 0)
    valid_mask = draw_valid_mask(jax.random.fold_in(streams_of[13], 71), 0)
    norm_gain = jnp.clip(1.0 + 0.1 * jax.random.normal(streams_of[3], (D,), jnp.float32), 0.5, 1.5).astype(jnp.bfloat16)
    norm_bias = bell_draw(streams_of[4], (D,), 0.3, 2.0)
    qkv_weight = bell_draw(streams_of[5], (D, 3, D), D ** -0.5, 0.125, ((0, 64), (2, 2)))
    qkv_bias = bell_draw(streams_of[6], (3, D), 0.5, 3.0, ((1, 2),))
    attn_out_weight = bell_draw(streams_of[7], (D, D), (max(D // 32, 1)) ** -0.5, 0.75, ((0, 64), (1, 2)))
    up_weight = bell_draw(streams_of[8], (D, FF), D ** -0.5, 0.125, ((0, 64), (1, 2)))
    up_bias = bell_draw(streams_of[9], (FF,), 0.5, 3.0, ((0, 2),))
    down_weight = bell_draw(streams_of[10], (D, FF), FF ** -0.5, 0.0625, ((0, 64), (1, 2)))
    out_bias = bell_draw(streams_of[11], (D,), 0.5, 3.0)
    grad_out = bell_draw(streams_of[12], (ROWS, LEN, D), 1.0, 6.0, ((0, 8), (1, 16)))
    return {"inputs": inputs, "segment_ids": segment_ids, "valid_mask": valid_mask, "norm_gain": norm_gain, "norm_bias": norm_bias, "qkv_weight": qkv_weight, "qkv_bias": qkv_bias, "attn_out_weight": attn_out_weight, "up_weight": up_weight, "up_bias": up_bias, "down_weight": down_weight, "out_bias": out_bias, "grad_out": grad_out}


EPSILON = 1e-05
MASKED = -1e+30
FULL = lax.Precision.HIGHEST

@jax.custom_vjp
def low(v):
    return lax.optimization_barrier(v.astype(jnp.bfloat16)).astype(jnp.float32)

@jax.custom_vjp
def low_back(v):
    return v

def low_keep(v):
    return (low(v), None)

def low_pass(kept, grad):
    return (grad,)

def back_keep(v):
    return (v, None)

def back_low(kept, grad):
    return (low(grad),)
low.defvjp(low_keep, low_pass)
low_back.defvjp(back_keep, back_low)

def gelu_tanh(value):
    return 0.5 * value * (1.0 + jnp.tanh(0.7978845608028654 * (value + 0.044715 * value * value * value)))

def positions_of(segment):
    index = jnp.arange(segment.shape[-1], dtype=jnp.int32)
    before = jnp.concatenate([segment[..., :1] - 1, segment[..., :-1]], -1)
    starts = jnp.where(segment != before, index, 0).astype(jnp.int32)
    return index - lax.cummax(starts, axis=segment.ndim - 1)

def rotary(value, place, sign):
    half = ROT // 2
    rates = 10000.0 ** (-2.0 * jnp.arange(half, dtype=jnp.float32) / ROT)
    angle = place.astype(jnp.float32)[..., None] * rates
    cosine = jnp.cos(angle)[..., None, :]
    sine = sign * jnp.sin(angle)[..., None, :]
    first = value[..., :half]
    second = value[..., half:ROT]
    return jnp.concatenate([first * cosine - second * sine, second * cosine + first * sine, value[..., ROT:]], -1)

def allowed_mask(seg_query, index_query, seg_key, index_key, valid_key):
    same = seg_query[..., :, None] == seg_key[..., None, :]
    causal = index_key[None, :] <= index_query[:, None]
    live = valid_key[..., None, :] == 1
    itself = index_key[None, :] == index_query[:, None]
    return same & causal & live | itself

def block_row(widened, segment, valid, gain, shift, triple_w, triple_b, out_w, up_w, up_b, down_w, bias_out):
    count = widened.shape[0]
    mean = lax.optimization_barrier(jnp.mean(widened, -1, keepdims=True))
    centred = widened - mean
    variance = lax.optimization_barrier(jnp.mean(centred * centred, -1, keepdims=True))
    normed = low(centred * lax.rsqrt(variance + EPSILON) * gain + shift)
    triple = low_back(jnp.einsum('td,djc->tjc', normed, triple_w, precision=FULL) + triple_b)
    place = positions_of(segment)
    query = low(rotary(triple[:, 0].reshape(count, H, HD), place, 1.0))
    key = low(rotary(triple[:, 1].reshape(count, H, HD), place, 1.0))
    value = low(triple[:, 2].reshape(count, H, HD))
    index = jnp.arange(count, dtype=jnp.int32)
    block = min(512, count)

    def attend(query_block, index_block, keys_all, values_all):
        scores = low_back(jnp.einsum('qhd,khd->hqk', query_block, keys_all, precision=FULL) * HD ** (-0.5))
        mask = allowed_mask(segment[index_block], index_block, segment, index, valid)
        scores = jnp.where(mask[None], scores, MASKED)
        top = lax.optimization_barrier(jnp.max(scores, -1, keepdims=True))
        weights = jnp.exp(scores - top)
        probs = low(weights / lax.optimization_barrier(jnp.sum(weights, -1, keepdims=True)))
        return jnp.einsum('hqk,khd->qhd', probs, values_all, precision=FULL)
    kept = jax.checkpoint(attend)
    heads = lax.map(lambda pair: kept(pair[0], pair[1], key, value), (query.reshape(count // block, block, H, HD), index.reshape(count // block, block)))
    heads = low(low_back(heads.reshape(count, H * HD)))
    hidden = low_back(jnp.dot(normed, up_w, precision=FULL) + up_b)
    act = low(gelu_tanh(hidden))
    attn = jnp.einsum('tc,ec->te', heads, out_w, precision=FULL)
    mlp = jnp.einsum('tf,ef->te', act, down_w, precision=FULL)
    return widened + attn + mlp + bias_out

def reference(inputs, segment_ids, valid_mask, norm_gain, norm_bias, qkv_weight, qkv_bias, attn_out_weight, up_weight, up_bias, down_weight, out_bias, grad_out):
    params = tuple((array.astype(jnp.float32) for array in (norm_gain, norm_bias, qkv_weight, qkv_bias, attn_out_weight, up_weight, up_bias, down_weight, out_bias)))

    def one_row(sums, row):
        row_in, row_seg, row_valid, row_grad = row

        def forward(widened, *weights):
            return block_row(widened, row_seg, row_valid, *weights)
        result, pull = jax.vjp(forward, row_in.astype(jnp.float32), *params)
        grads = pull(row_grad.astype(jnp.float32))
        new_sums = tuple((total + extra for total, extra in zip(sums, grads[1:])))
        return (new_sums, (result.astype(jnp.bfloat16), grads[0]))
    start = tuple((jnp.zeros(array.shape, jnp.float32) for array in params))
    sums, (output, grad_inputs) = lax.scan(one_row, start, (inputs, segment_ids, valid_mask, grad_out))
    return (output, grad_inputs, sums[0], sums[1], sums[2], sums[3], sums[4], sums[5], sums[6], sums[7], sums[8])
```

```python
import functools

import jax
import jax.numpy as jnp
import numpy as np
from jax import lax
from jax.experimental import pallas as pl
from jax.experimental.pallas import tpu as pltpu
from jax.sharding import PartitionSpec as P


HD = 64
ROT = 32
EPSILON = 1e-05
MASKED = -1e30
MESH = pl.DeviceIdType.MESH
BF = jnp.bfloat16
F32 = jnp.float32

D = 2048
T = 2048
CQ = 128
CF = 512
CI = 3 * CQ + CF
CO = CQ + CF
CS = CI + 256
BLK = 256
NB = T // BLK
QB = 512
NQ = T // QB
VMEM_LIMIT = 65400 * 1024
SLOTS = 224


def dot(a, b):
    return lax.dot_general(a, b, (((1,), (0,)), ((), ())), preferred_element_type=F32)


def dot_nt(a, b):
    return lax.dot_general(a, b, (((1,), (1,)), ((), ())), preferred_element_type=F32)


def loop(n, body, events=()):
    def run(i, carry):
        body(i)
        for when, event in events:
            pl.when(i == when)(event)
        return carry

    lax.fori_loop(0, n, run, 0)


def pieces(n, step, body):
    loop(n // step, lambda i: body(pl.multiple_of(i * step, step)))


class Net:
    def __init__(self, send_sems, recv_sems, credits):
        self.credits = credits
        self.dp, self.seq, self.branch = (lax.axis_index(n) for n in ("dp", "seq", "branch"))
        self.x, self.yl = lax.rem(self.dp, 4), lax.div(self.dp, 4)
        self.z, self.core = lax.div(self.seq, 2), lax.rem(self.seq, 2)
        self.send_sems, self.recv_sems = send_sems, recv_sems
        self.slots, self.sent = {}, []
        self.right, self.left = self.at(dz=1), self.at(dz=3)
        self.sib, self.mate = self.at(dc=1), self.at(db=1)
        self.xright, self.xleft, self.ymate = self.at(dx=1), self.at(dx=3), self.at(dy=1)

    def at(self, dx=0, dy=0, dz=0, dc=0, db=0):
        x, yl = lax.rem(self.x + dx, 4), lax.rem(self.yl + dy, 2)
        z, core = lax.rem(self.z + dz, 4), lax.rem(self.core + dc, 2)
        return (yl * 4 + x, z * 2 + core, lax.rem(self.branch + db, 2))

    def seq_peer(self, d):
        return (self.dp, lax.rem(self.seq + d, 8), self.branch)

    def dp_peer(self, d):
        return (lax.rem(self.dp + d, 8), self.seq, self.branch)

    def greet(self, devices):
        barrier = pltpu.get_barrier_semaphore()
        for device in devices:
            pl.semaphore_signal(barrier, inc=1, device_id=device, device_id_type=MESH)
        return lambda: pl.semaphore_wait(barrier, len(devices))

    def slot(self, key):
        return self.slots.setdefault(key, len(self.slots))

    def copy(self, key, src, dst, to):
        index = self.slot(key)
        return pltpu.make_async_remote_copy(
            src_ref=src,
            dst_ref=dst,
            send_sem=self.send_sems.at[index],
            recv_sem=self.recv_sems.at[index],
            device_id=to,
            device_id_type=MESH,
        )

    def send(self, key, src, dst, to, like=None):
        self.copy(key, src, dst, to).start()
        self.sent.append((key, src if like is None else like))

    def recv(self, key, dst):
        self.copy(key, dst, dst, self.sib).wait_recv()

    def drain(self, tag=None):
        for key, like in self.sent:
            if tag is None or key[0] == tag:
                self.copy(key, like, like, self.sib).wait_send()
        self.sent = [(key, like) for key, like in self.sent if tag is not None and key[0] != tag]

    def allow(self, index, devices):
        for device in devices:
            pl.semaphore_signal(self.credits.at[index], inc=1, device_id=device, device_id_type=MESH)


class Local:
    def __init__(self, sems):
        self.sems, self.count, self.open = sems, 0, []

    def start(self, src, dst, keep=True):
        copy = pltpu.make_async_copy(src, dst, self.sems.at[self.count])
        self.count += 1
        copy.start()
        if keep:
            self.open.append(copy)
        return copy

    def finish(self):
        for copy in self.open:
            copy.wait()
        self.open = []


class Gather:
    def __init__(self, net, tag, buf, rows, n, ring, right, left, mate, sib=None, across=None):
        self.net, self.tag, self.buf, self.n = net, tag, buf, n
        self.right, self.left, self.mate, self.sib, self.across = right, left, mate, sib, across
        self.starts = {
            (dr, rel, other): rows(lax.rem(ring + dr, 4), rel, other)
            for dr in range(4)
            for rel in (0, 1)
            for other in ((False, True) if sib is not None else (False,))
        }

    def view(self, dr, rel, lo=0, n=None, other=False):
        start = self.starts[dr, rel, other] + lo
        return self.buf.at[pl.ds(pl.multiple_of(start, 16), self.n if n is None else n)]

    def _send(self, key, view, to):
        self.net.send((self.tag,) + key, view, view, to, self.buf.at[pl.ds(0, view.shape[0])])

    def _recv(self, key, view):
        self.net.recv((self.tag,) + key, view)

    def to_sib(self, dr, rel):
        if self.sib is not None:
            self._send(("s", dr, rel), self.view(dr, rel), self.sib)

    def start_mate(self):
        self._send(("m",), self.view(0, 0), self.mate)

    def start_ring(self, rel=0):
        view = self.view(0, rel)
        self._send(("r", rel), view, self.right)
        self._send(("l", rel), view, self.left)
        if self.across is not None:
            self._send(("a", rel), view, self.across)
        self.to_sib(0, rel)

    def from_mate(self):
        self._recv(("m",), self.view(0, 1))
        self.start_ring(1)

    def direct(self):
        for rel in (0, 1):
            for key, dr in (("r", 3), ("l", 1), ("a", 2)):
                self._recv((key, rel), self.view(dr, rel))

    def near(self, rel):
        half = self.n // 2
        self._recv(("r", rel), self.view(3, rel))
        self._send(("rr", rel), self.view(3, rel, 0, half), self.right)
        self.to_sib(3, rel)
        self._recv(("l", rel), self.view(1, rel))
        self._send(("ll", rel), self.view(1, rel, half, half), self.left)
        self.to_sib(1, rel)

    def far(self, rel):
        half = self.n // 2
        self._recv(("rr", rel), self.view(2, rel, 0, half))
        self._recv(("ll", rel), self.view(2, rel, half, half))
        self.to_sib(2, rel)

    def from_sib(self, dr):
        for rel in (0, 1):
            self._recv(("s", dr, rel), self.view(dr, rel, other=True))


def token_rows(net):
    def rows(ring, rel, other):
        core = lax.rem(net.core + (1 if other else 0), 2)
        return (ring * 2 + core) * 256 + lax.rem(net.branch + rel, 2) * 128

    return rows


def weight_rows(net):
    def rows(ring, rel, other):
        return (lax.rem(net.yl + rel, 2) * 4 + ring) * 256

    return rows


def norm_stats(x):
    mean = jnp.mean(x, -1, keepdims=True)
    centred = x - mean
    variance = jnp.mean(centred * centred, -1, keepdims=True)
    rstd = lax.rsqrt(variance + EPSILON)
    return centred * rstd, rstd


def roll_lanes(x, shift):
    return pltpu.roll(x, shift % x.shape[1], 1)


def rotate(x, cos, sine):
    lane = lax.broadcasted_iota(jnp.int32, x.shape, 1) & (HD - 1)
    return x * cos + jnp.where(lane < ROT // 2, roll_lanes(x, -16), roll_lanes(x, 16)) * sine


def scores_of(keys, queries, key_ids, seg_row, behind=None):
    s = dot_nt(keys, queries)
    allowed = jnp.concatenate([key_ids] * (2 * QB // 128), 1) == seg_row
    if behind is not None:
        key_at = lax.broadcasted_iota(jnp.int32, s.shape, 0) + behind
        query_at = lax.broadcasted_iota(jnp.int32, s.shape, 1) & (QB - 1)
        allowed = (allowed & (key_at <= query_at)) | (key_at == query_at)
    return jnp.where(allowed, s, MASKED)


class Scatter:
    def __init__(self, net, tag, view, near, far, mate_buf, n, right, left, mate):
        self.net, self.tag, self.view, self.near, self.far, self.mate_buf = net, tag, view, near, far, mate_buf
        self.right, self.left, self.mate, self.n, self.half = right, left, mate, n, n // 2
        self.like, self.whole = far(0, 0), mate_buf

    def _send(self, key, src, dst, to):
        self.net.send((self.tag,) + key, src, dst, to, self.like)

    def _recv(self, key):
        self.net.recv((self.tag,) + key, self.like)

    def begin(self, rel):
        half = self.half
        self._send(("rr", rel), self.view(2, rel, 0, half), self.far(0, rel), self.right)
        self._send(("ll", rel), self.view(2, rel, half, half), self.far(1, rel), self.left)

    def begin_near(self, rel):
        half = self.half
        self._send(("rb", rel), self.view(1, rel, half, half), self.near(0, rel).at[pl.ds(half, half)], self.right)
        self._send(("lt", rel), self.view(3, rel, 0, half), self.near(1, rel).at[pl.ds(0, half)], self.left)

    def middle(self, rel):
        for key, dr, way, lo, done, to in (
            ("rr", 1, 0, 0, "rt", self.right),
            ("ll", 3, 1, self.half, "lb", self.left),
        ):
            self._recv((key, rel))

            step = 32 if self.half % 32 == 0 else 16

            def add(first):
                part = self.view(dr, rel, lo + first, step)
                part[...] = (part[...].astype(F32) + self.far(way, rel)[pl.ds(first, step), :].astype(F32)).astype(BF)

            pieces(self.half, step, add)
            view = self.view(dr, rel, lo, self.half)
            self._send((done, rel), view, self.near(way, rel).at[pl.ds(lo, self.half)], to)

    def end(self, rel):
        for key in ("rb", "rt", "lt", "lb"):
            self._recv((key, rel))

        def add(first):
            view, at = self.view(0, rel, first, 32), pl.ds(first, 32)
            total = view[...].astype(F32) + self.near(0, rel)[at, :].astype(F32) + self.near(1, rel)[at, :].astype(F32)
            view[...] = total.astype(BF)

        pieces(self.n, 32, add)

    def to_mate(self):
        self.net.send(("m" + self.tag,), self.view(0, 1, 0, self.n), self.whole, self.mate, self.whole)

    def last(self):
        self.net.recv(("m" + self.tag,), self.whole)

    def total(self, first, n):
        return self.view(0, 0, first, n)[...].astype(F32) + self.mate_buf[pl.ds(first, n), :].astype(F32)


class AllSum:
    def __init__(self, net, tag, vec, seq_buf, dp_buf, mate_buf):
        self.net, self.tag, self.vec = net, tag, vec
        self.seq_buf, self.dp_buf, self.mate_buf = seq_buf, dp_buf, mate_buf

    def _spread(self, key, buf, me, peer):
        buf[me] = self.vec[...]
        for d in range(1, 8):
            self.net.send((self.tag, key, d), buf.at[me], buf.at[me], peer(d))

    def _total(self, key, buf, me):
        for d in range(1, 8):
            self.net.recv((self.tag, key, d), buf.at[lax.rem(me + 8 - d, 8)])
        total = buf[0]
        for s in range(1, 8):
            total = total + buf[s]
        self.vec[...] = total

    def start(self):
        self._spread("d", self.dp_buf, self.net.dp, self.net.dp_peer)

    def second(self):
        self._total("d", self.dp_buf, self.net.dp)
        self.net.send((self.tag, "b"), self.vec, self.mate_buf, self.net.mate)

    def third(self):
        self.net.recv((self.tag, "b"), self.mate_buf)
        self.seq_buf[self.net.seq] = self.vec[...] + self.mate_buf[...]
        mine = self.seq_buf.at[self.net.seq]
        for d in range(1, 8):
            self.net.send((self.tag, "q", d), mine, mine, self.net.seq_peer(d))

    def done(self):
        me = self.net.seq
        for d in range(1, 8):
            self.net.recv((self.tag, "q", d), self.seq_buf.at[lax.rem(me + 8 - d, 8)])
        total = self.seq_buf[0]
        for s in range(1, 8):
            total = total + self.seq_buf[s]
        return total


class PairFirst(Scatter):
    def give(self, dr):
        for src, dst in zip(self._cuts(dr), self.mate_buf(dr)):
            self.net.send(("p" + self.tag, dr, src[1]), src[0], dst, self.mate)

    def _cuts(self, dr):
        refs = self.mate_buf(dr)
        n = self.n // len(refs)
        return [(self.view(dr, 1, i * n, n), i) for i in range(len(refs))]

    def take(self, dr):
        for i, ref in enumerate(self.mate_buf(dr)):
            self.net.recv(("p" + self.tag, dr, i), ref)
            n = self.n // len(self.mate_buf(dr))

            def add(first, i=i, n=n, ref=ref):
                mine = self.view(dr, 0, i * n + first, 16)
                mine[...] = (mine[...].astype(F32) + ref[pl.ds(first, 16), :].astype(F32)).astype(BF)

            pieces(n, 16, add)

    def total(self, first, n):
        return self.view(0, 0, first, n)[...].astype(F32)


def turn_weights(scatter, send_buf):
    def turn(first):
        send_buf[:, pl.ds(first, 128)] = scatter.total(first, 128).T.astype(BF)

    pieces(scatter.n, 128, turn)


def send_weights(net, tag, width, send_buf, recv_buf):
    columns = pl.ds(0, width)
    for d in range(1, 8):
        to = lax.rem(net.seq + d, 8)
        src = send_buf.at[pl.ds(pl.multiple_of(to * 32, 32), 32), columns]
        net.send((tag, d), src, recv_buf.at[net.seq], net.seq_peer(d))
    recv_buf[net.seq] = send_buf[pl.ds(pl.multiple_of(net.seq * 32, 32), 32), columns]


def receive_weights(net, tag, recv_buf):
    for d in range(1, 8):
        net.recv((tag, d), recv_buf.at[lax.rem(net.seq + 8 - d, 8)])


def ring_step(t):
    return jnp.where(t == 0, 2, jnp.where(t == 1, 1, jnp.where(t == 2, 3, 0)))


def block_kernel(
    x_in, go_in, qkv_in, up_in, att_in, down_in, seg_in, valid_in, vectors_in, qkv_b, rates_in,
    n_out, output_ref, ginp_ref, sums_ref, bias_ref, wo_ref, wu_ref, wq_ref,
    n_buf, g_buf, sib_buf, wq, wu, wo, tab, kid, segs, qst, k, v, kt, vt, mix, mixt, dgel, ot,
    dost, dk, dv, lse, delta, m_ref, l_ref, acc_ref, bias,
    near, far, mate_buf, gw, wnear, wfar, wmate, wsend, wrecv_o, wrecv_u, wrecv_q,
    bsum, bdp, bseq, vec, vseq, vdp, vmate,
    send_sems, recv_sems, local_sems, credits,
):
    net, local = Net(send_sems, recv_sems, credits), Local(local_sems)
    gain_in, shift_in, ob_in, up_b = (
        vectors_in.at[:, pl.ds(first, width)] for first, width in ((0, D), (D, D), (2 * D, D), (3 * D, 4096))
    )
    rows = token_rows(net)
    own = pl.ds(pl.multiple_of(rows(net.z, 0, False), 128), 128)
    get_x = local.start(x_in, vt, False)
    get_g = local.start(go_in, g_buf.at[own], False)
    dp_peers = [net.dp_peer(d) for d in range(1, 8)]
    all_here = net.greet([net.seq_peer(d) for d in range(1, 8)] + dp_peers + [net.mate])

    groups = (
        ("q", wq, [(qkv_in.at[j], CQ, j * CQ) for j in range(3)]),
        ("u", wu, [(up_in, CF, 0)]),
        ("o", wo, [(att_in, CQ, 0), (down_in, CF, CQ)]),
    )
    mine = pl.ds(pl.multiple_of(net.dp * 256 + net.seq * 32, 32), 32)

    def cuts(to, group):
        name, buf, parts = group
        return [
            (src.at[:, pl.ds(pl.multiple_of(to * width, 128), width)], buf.at[mine, pl.ds(first, width)])
            for src, width, first in parts
        ]

    own_parts = [local.start(src, dst, False) for group in groups for src, dst in cuts(net.seq, group)]

    def send_pieces(group):
        for d in range(1, 8):
            for src, dst in cuts(lax.rem(net.seq + d, 8), group):
                net.copy(("p" + group[0], d), src, dst, net.seq_peer(d)).start()
            net.sent.append((("p" + group[0], d), group[1].at[mine]))

    def receive_pieces(group):
        for d in range(1, 8):
            sender = net.dp * 256 + lax.rem(net.seq + 8 - d, 8) * 32
            net.recv(("p" + group[0], d), group[1].at[pl.ds(pl.multiple_of(sender, 32), 32)])

    get_x.wait()

    def norm(first):
        xhat, unused = norm_stats(vt[pl.ds(first, 32), :].astype(F32))
        at = pl.ds(pl.multiple_of(rows(net.z, 0, False) + first, 32), 32)
        n_buf[at, :] = (xhat * gain_in[...].astype(F32) + shift_in[...].astype(F32)).astype(BF)

    pieces(128, 32, norm)
    ag_n = Gather(net, "n", n_buf, rows, 128, net.z, net.right, net.left, net.mate, net.sib)
    ag_g = Gather(net, "g", g_buf, rows, 128, net.z, net.right, net.left, net.mate, net.sib)
    wrows = weight_rows(net)
    ag_q, ag_u, ag_o = (
        Gather(net, name, buf, wrows, 256, net.x, net.xright, net.xleft, net.ymate) for name, buf, parts in groups
    )
    all_here()
    send_pieces(groups[0])
    ag_n.start_mate()
    ag_n.start_ring()
    for copy in own_parts:
        copy.wait()
    receive_pieces(groups[0])
    ag_q.start_mate()
    ag_q.start_ring()

    for j in range(3):
        bias[:, j * CQ : (j + 1) * CQ] = qkv_b[j : j + 1, pl.ds(pl.multiple_of(net.seq * CQ, CQ), CQ)].astype(F32)
    bias[:, 3 * CQ :] = up_b[:, pl.ds(pl.multiple_of(net.seq * CF, CF), CF)].astype(F32)
    seg = seg_in[...].astype(F32)
    valid = valid_in[...].astype(F32)
    starts = [jnp.sum((seg < d).astype(F32), 1, keepdims=True) for d in range(1, 5)]
    for i in range(NQ):
        part_seg = seg[:, i * QB : (i + 1) * QB]
        segs[i] = jnp.concatenate([part_seg, part_seg], 1)
    key_seg = jnp.where(valid == 1.0, seg, -1.0)
    for i in range(T // 128):
        at = slice(i * 128, (i + 1) * 128)
        kid[at, :] = jnp.broadcast_to(key_seg[:, at], (128, 128)).T
        seg_col = jnp.broadcast_to(seg[:, at], (128, 128)).T
        first = jnp.zeros((128, 128), F32)
        for d in range(1, 5):
            first = jnp.where(seg_col >= d, jnp.broadcast_to(starts[d - 1], (128, 128)), first)
        index = (lax.broadcasted_iota(jnp.int32, (128, 128), 0) + i * 128).astype(F32)
        tab[0, at, :] = index - first

    def table(i):
        at = pl.ds(pl.multiple_of(i * BLK, BLK), BLK)
        angle = tab[0, at, :] * rates_in[...]
        lane = lax.broadcasted_iota(jnp.int32, (BLK, 128), 1) & (HD - 1)
        sine = jnp.sin(angle)
        tab[0, at, :] = jnp.where(lane < ROT, jnp.cos(angle), 1.0)
        tab[1, at, :] = jnp.where(lane < ROT // 2, -sine, jnp.where(lane < ROT, sine, 0.0))

    loop(NB, table)

    def entry(i):
        at = pl.ds(pl.multiple_of(i * BLK, BLK), BLK)
        t = dot(n_buf[at, :], wq[...]) + bias[:, : 3 * CQ]
        cos, sine = tab[0, at, :], tab[1, at, :]
        lane = lax.broadcasted_iota(jnp.int32, (BLK, CQ), 1)
        q = rotate(t[:, :CQ], cos, sine).astype(BF).astype(F32) * HD ** (-0.5)
        block, first = lax.div(i, 2), pl.multiple_of(lax.rem(i, 2) * BLK, BLK)
        qst[block, pl.ds(first, BLK), :] = jnp.where(lane < HD, q, 0.0).astype(BF)
        qst[block, pl.ds(first + QB, BLK), :] = jnp.where(lane < HD, 0.0, q).astype(BF)
        key = rotate(t[:, CQ : 2 * CQ], cos, sine)
        k[at, :] = key.astype(BF)
        kt[:, at] = key.T.astype(BF)
        value = t[:, 2 * CQ :]
        v[at, :] = value.astype(BF)
        vt[:, at] = value.T.astype(BF)

    def up_entry(i):
        at = pl.ds(pl.multiple_of(i * BLK, BLK), BLK)
        h = dot(n_buf[at, :], wu[...]) + bias[:, 3 * CQ :]
        square = h * h
        th = jnp.tanh(0.7978845608028654 * h * (1.0 + 0.044715 * square))
        act = 0.5 * h * (1.0 + th)
        slope = 0.5 * (1.0 + th) + 0.5 * h * (1.0 - th * th) * (
            0.7978845608028654 * (1.0 + 3 * 0.044715 * square)
        )
        mix[at, CQ:CO] = act.astype(BF)
        mixt[CQ:CO, at] = act.T.astype(BF)
        for part in (0, 1):
            dgel[lax.div(i, 2), lax.rem(i, 2), part * BLK : (part + 1) * BLK, :] = slope[
                :, part * BLK : (part + 1) * BLK
            ].astype(BF)

    def on_place(dr, work):
        first = lax.rem(net.z + dr, 4) * 2
        loop(2, lambda t: work(first + t))

    get_g.wait()
    ag_q.from_mate()
    ag_n.from_mate()
    send_pieces(groups[1])
    send_pieces(groups[2])
    ag_q.near(0)
    ag_n.near(0)
    ag_q.near(1)
    ag_g.start_mate()
    ag_q.far(0)
    ag_q.far(1)
    ag_n.from_sib(0)
    on_place(0, entry)
    receive_pieces(groups[1])
    ag_u.start_mate()
    ag_u.start_ring()
    ag_n.near(1)
    ag_n.from_sib(3)
    on_place(3, entry)
    ag_n.from_sib(1)
    on_place(1, entry)
    ag_u.from_mate()
    receive_pieces(groups[2])
    ag_o.start_mate()
    ag_o.start_ring()
    ag_n.far(0)
    ag_u.near(0)
    ag_n.far(1)
    ag_g.start_ring()
    ag_g.from_mate()
    ag_n.from_sib(2)
    on_place(2, entry)
    park = local.start(n_buf, n_out, False)

    def attend(i):
        at = pl.ds(pl.multiple_of(i * QB, QB), QB)
        queries, seg_row = qst[i], segs[i]

        def keys_at(j):
            return pl.ds(pl.multiple_of(j * BLK, BLK), BLK)

        def step(j, behind=None):
            kat = keys_at(j)
            s = scores_of(k[kat, :], queries, kid[kat, :], seg_row, behind)
            old = m_ref[...]
            top = jnp.maximum(old, jnp.max(s, 0, keepdims=True))
            fade = jnp.exp(old - top)
            p = jnp.exp(s - top)
            m_ref[...] = top
            l_ref[...] = l_ref[...] * fade + jnp.sum(p, 0, keepdims=True)
            acc_ref[...] = acc_ref[...] * fade + dot(vt[:, kat], p.astype(BF))

        kat = keys_at(2 * i)
        s = scores_of(k[kat, :], queries, kid[kat, :], seg_row, 0)
        top = jnp.max(s, 0, keepdims=True)
        p = jnp.exp(s - top)
        m_ref[...] = top
        l_ref[...] = jnp.sum(p, 0, keepdims=True)
        acc_ref[...] = dot(vt[:, kat], p.astype(BF))
        step(2 * i + 1, BLK)
        loop(2 * i, step)
        lse[i] = m_ref[...] + jnp.log(l_ref[...])
        both = acc_ref[...] / l_ref[...]
        heads = jnp.concatenate([both[:HD, :QB], both[HD:, QB:]], 0)
        ot[:, at] = heads
        mixt[:CQ, at] = heads.astype(BF)
        mix[at, :CQ] = heads.T.astype(BF)

    loop(NQ, attend, ((0, lambda: ag_u.near(1)), (0, ag_o.from_mate), (2, lambda: ag_u.far(0)), (2, lambda: ag_u.far(1))))
    ag_o.near(0)
    get_x = local.start(x_in, vt, False)
    loop(NB, up_entry, ((0, lambda: ag_o.near(1)), (2, lambda: ag_g.near(0)), (3, lambda: ag_g.near(1))))
    ag_o.far(0)
    ag_o.far(1)

    park.wait()
    net.drain("n")

    def chunk_view(buf):
        starts = {(dr, rel): rows(lax.rem(net.z + dr, 4), rel, False) for dr in range(4) for rel in (0, 1)}

        def view(dr, rel, lo, n):
            return buf.at[pl.ds(pl.multiple_of(starts[dr, rel] + lo, 16), n)]

        return view

    def block_rows(dr, other):
        core = lax.rem(net.core + (1 if other else 0), 2)
        return pl.ds(pl.multiple_of((lax.rem(net.z + dr, 4) * 2 + core) * 256, 256), 256)

    def partial_blocks(tag, buf, product, hooks):
        def other(dr):
            at = block_rows(dr, True)
            buf[at, :] = product(at).astype(BF)
            net.send((tag, dr), buf.at[at], sib_buf.at[dr], net.sib)

        def own(dr):
            at = block_rows(dr, False)
            value = product(at)
            net.recv((tag, dr), sib_buf.at[dr])
            buf[at, :] = (value + sib_buf[dr].astype(F32)).astype(BF)

        other(2)
        other(1)
        own(2)
        hooks[0]()
        other(3)
        hooks[1]()
        own(1)
        other(0)
        own(3)
        hooks[2]()
        own(0)

    def near_at(way, rel):
        return near.at[way, rel]

    def far_at(way, rel):
        return far.at[way, rel]

    out_view = chunk_view(n_buf)
    rs_out = Scatter(net, "t1", out_view, near_at, far_at, mate_buf, 128, net.right, net.left, net.mate)

    def nothing():
        pass

    def gather_end():
        ag_g.far(0)
        ag_g.far(1)
        for rel in (1, 0):
            rs_out.begin(rel)
            rs_out.begin_near(rel)

    partial_blocks("s1", n_buf, lambda at: dot_nt(mix[at, :CO], wo[...]), (nothing, nothing, gather_end))
    net.allow(0, [net.sib])
    for dr in range(4):
        ag_g.from_sib(dr)

    bsum[...] = jnp.zeros_like(bsum)

    def sum_rows(i):
        at = pl.ds(pl.multiple_of(i * BLK, BLK), BLK)
        mine = g_buf[at, pl.ds(pl.multiple_of(net.seq * 256, 256), 256)]
        bsum[:, CI:] += jnp.sum(mine.astype(F32), 0, keepdims=True)

    loop(NB, sum_rows)

    def back(i):
        at = pl.ds(pl.multiple_of(i * BLK, BLK), BLK)
        t = dot(g_buf[at, :], wo[...])
        lane = lax.broadcasted_iota(jnp.int32, (BLK, CQ), 1)
        do = t[:, :CQ].astype(BF).astype(F32)
        block, first = lax.div(i, 2), pl.multiple_of(lax.rem(i, 2) * BLK, BLK)
        dost[block, pl.ds(first, BLK), :] = jnp.where(lane < HD, do, 0.0).astype(BF)
        dost[block, pl.ds(first + QB, BLK), :] = jnp.where(lane < HD, 0.0, do).astype(BF)
        terms = do.T * ot[:, at]
        delta[block, :, pl.ds(first, BLK)] = jnp.sum(terms[:HD], 0, keepdims=True)
        delta[block, :, pl.ds(first + QB, BLK)] = jnp.sum(terms[HD:], 0, keepdims=True)
        for part in (0, 1):
            slope = dgel[lax.div(i, 2), lax.rem(i, 2), part * BLK : (part + 1) * BLK, :].astype(F32)
            grad = t[:, CQ + part * BLK : CQ + (part + 1) * BLK] * slope
            mix[at, 3 * CQ + part * BLK : 3 * CQ + (part + 1) * BLK] = grad.astype(BF)

    loop(NB, back)
    net.drain("o")
    net.allow(5, [net.xleft, net.xright, net.ymate])

    def weight_scatter(tag, buf, near_of, far_of, last_buf, width):
        return Scatter(
            net, tag, lambda dr, rel, lo, n: buf.at[dr, rel, pl.ds(lo, n)], near_of, far_of, last_buf, width,
            net.xright, net.xleft, net.ymate,
        )

    def sized(buf, n):
        return lambda way, rel: buf.at[way, rel, pl.ds(0, n)]

    def weight_chunks(scatter, buf, first, features):
        width = scatter.n

        def body(t):
            dr, rel = ring_step(lax.div(t, 2)), 1 - lax.rem(t, 2)
            dp = lax.rem(net.yl + rel, 2) * 4 + lax.rem(net.x + dr, 4)
            columns = pl.ds(pl.multiple_of(dp * 256, 256), 256)
            buf[dr, rel, :width] = dot(mixt[first : first + width, :], features[:, columns]).astype(BF)

        loop(
            NB,
            body,
            (
                (0, lambda: scatter.begin(1)), (1, lambda: scatter.begin(0)), (4, lambda: scatter.begin_near(1)),
                (5, lambda: scatter.begin_near(0)),
            ),
        )

    rs_o = weight_scatter("w1", gw, sized(wnear, CO), sized(wfar, CO // 2), wmate, CO)
    weight_chunks(rs_o, gw, 0, g_buf)
    net.drain("g")
    reload = local.start(n_out, g_buf, False)

    def put(at, first, value):
        width = value.shape[1]
        rounded = value.astype(BF)
        mix[at, first : first + width] = rounded
        mixt[first : first + width, at] = value.T.astype(BF)
        return jnp.sum(rounded.astype(F32), 0, keepdims=True)


    def turn_hidden(i):
        at = pl.ds(pl.multiple_of(i * BLK, BLK), BLK)
        grad = mix[at, 3 * CQ :].astype(F32)
        mixt[3 * CQ :, at] = grad.T.astype(BF)
        bsum[:, 3 * CQ : CI] += jnp.sum(grad, 0, keepdims=True)

    loop(NB, turn_hidden)
    reload.wait()
    rs_u = weight_scatter(
        "w2",
        dgel,
        lambda way, rel: wo.at[pl.ds((2 * way + rel) * CF, CF), pl.ds(0, 256)],
        lambda way, rel: wo.at[pl.ds((2 * way + rel) * 256, 256), pl.ds(256, 256)],
        wo.at[pl.ds(2 * CF, CF), pl.ds(256, 256)],
        CF,
    )
    pl.semaphore_wait(credits.at[5], 3)
    weight_chunks(rs_u, dgel, 3 * CQ, g_buf)

    def block(i):
        at = pl.ds(pl.multiple_of(i * QB, QB), QB)
        queries, dos, seg_row, log_total, shift = qst[i], dost[i], segs[i], lse[i], delta[i]
        acc_ref[...] = jnp.zeros_like(acc_ref)

        def tile(j, behind=None):
            kat = pl.ds(pl.multiple_of(j * BLK, BLK), BLK)
            s = scores_of(k[kat, :], queries, kid[kat, :], seg_row, behind)
            p = jnp.exp(s - log_total)
            ds = (p * (dot_nt(v[kat, :], dos) - shift)).astype(BF)
            acc_ref[...] += dot(kt[:, kat], ds)
            return kat, dot(p.astype(BF), dos), dot(ds, queries)

        for c in (0, 1):
            kat, add_v, add_k = tile(2 * i + c, c * BLK)
            dv[kat, :] = add_v
            dk[kat, :] = add_k

        def step(j):
            kat, add_v, add_k = tile(j)
            dv[kat, :] += add_v
            dk[kat, :] += add_k

        loop(2 * i, step)
        dq = jnp.concatenate([acc_ref[:HD, :QB], acc_ref[HD:, QB:]], 0).T * HD ** (-0.5)
        bsum[:, :CQ] += put(at, 0, rotate(dq, tab[0, at, :], -tab[1, at, :]))

    loop(
        NQ,
        block,
        (
            (1, lambda: rs_out.middle(1)), (2, lambda: rs_out.middle(0)), (2, lambda: rs_o.middle(1)),
            (2, lambda: rs_o.middle(0)), (3, lambda: rs_out.end(1)), (3, rs_out.to_mate), (3, lambda: rs_o.end(1)),
            (3, rs_o.to_mate),
        ),
    )

    def finish_keys(i):
        at = pl.ds(pl.multiple_of(i * BLK, BLK), BLK)
        bsum[:, CQ : 2 * CQ] += put(at, CQ, rotate(dk[at, :], tab[0, at, :], -tab[1, at, :]))
        bsum[:, 2 * CQ : 3 * CQ] += put(at, 2 * CQ, dv[at, :])

    loop(NB, finish_keys)

    rs_o.end(0)
    net.allow(2, [net.xleft, net.xright])
    rs_out.end(0)
    net.allow(1, [net.left, net.right])
    net.allow(6, [net.mate])
    net.drain("s1")
    net.drain("t1")
    pl.semaphore_wait(credits.at[0], 1)
    pl.semaphore_wait(credits.at[1], 2)
    rs_in = Scatter(
        net,
        "t2",
        out_view,
        lambda way, rel: near.at[way, rel, pl.ds(0, 96)],
        lambda way, rel: far.at[way, rel, pl.ds(0, 48)],
        mate_buf.at[pl.ds(0, 96)],
        96,
        net.right,
        net.left,
        net.mate,
    )
    from_mate = {
        2: [near.at[0, 1, pl.ds(96, 32)]],
        1: [near.at[1, 1, pl.ds(96, 32)]],
        3: [far.at[0, 1, pl.ds(48, 16)], far.at[1, 1, pl.ds(48, 16)]],
        0: [mate_buf.at[pl.ds(96, 32)]],
    }
    rs_pair = PairFirst(
        net,
        "t3",
        lambda dr, rel, lo, n: out_view(dr, rel, lo + 96, n),
        lambda way, rel: near.at[way, rel, pl.ds(96, 32)],
        lambda way, rel: far.at[way, rel, pl.ds(48, 16)],
        from_mate.get,
        32,
        net.right,
        net.left,
        net.mate,
    )
    pl.semaphore_wait(credits.at[6], 1)

    def begin():
        rs_in.begin(1)
        rs_in.begin(0)
        rs_pair.give(2)

    def begin_up():
        rs_u.middle(1)
        rs_u.middle(0)

    def output_ends():
        rs_in.begin_near(1)
        rs_in.begin_near(0)
        rs_pair.give(1)
        rs_pair.give(3)
        rs_out.last()
        get_x.wait()

        def residual(first):
            at = pl.ds(first, 32)
            kt[at, :] = (vt[at, :].astype(F32) + rs_out.total(first, 32) + ob_in[...].astype(F32)).astype(BF)

        pieces(128, 32, residual)
        net.drain("mt1")
        net.allow(3, [net.mate])

    partial_blocks(
        "s2",
        n_buf,
        lambda at: dot_nt(mix[at, : 3 * CQ], wq[...]) + dot_nt(mix[at, 3 * CQ :], wu[...]),
        (begin, begin_up, output_ends),
    )
    put_output = local.start(kt, output_ref, False)
    pl.semaphore_wait(credits.at[3], 1)
    rs_pair.take(2)
    rs_pair.begin(0)
    rs_o.last()
    turn_weights(rs_o, wsend)
    net.drain("w1")
    net.drain("mw1")
    net.allow(4, [net.ymate])
    pl.semaphore_wait(credits.at[2], 2)
    rs_q = weight_scatter(
        "w3", gw, sized(wnear, 3 * CQ), sized(wfar, 3 * CQ // 2), wmate.at[pl.ds(0, 3 * CQ)], 3 * CQ
    )
    weight_chunks(rs_q, gw, 0, g_buf)
    rs_in.middle(1)
    rs_in.middle(0)
    rs_u.end(1)
    rs_u.to_mate()
    rs_u.end(0)
    rs_pair.take(1)
    rs_pair.take(3)
    rs_pair.begin_near(0)
    rs_pair.give(0)

    bdp[net.dp] = bsum[...]
    for d in range(1, 8):
        net.send(("b", d), bdp.at[net.dp], bdp.at[net.dp], net.dp_peer(d))
    put_output.wait()
    get_go = local.start(go_in, kt, False)
    rs_pair.middle(0)
    rs_q.middle(1)
    rs_q.middle(0)
    rs_in.end(1)
    rs_in.to_mate()
    rs_in.end(0)
    rs_pair.take(0)
    rs_pair.end(0)
    send_weights(net, "xo", CO, wsend, wrecv_o)
    for d in range(1, 8):
        net.recv(("b", d), bdp.at[lax.rem(net.dp + 8 - d, 8)])
    total = bdp[0]
    for s in range(1, 8):
        total = total + bdp[s]
    bseq[net.seq] = total
    for d in range(1, 8):
        net.send(("c", d), bseq.at[net.seq], bseq.at[net.seq], net.seq_peer(d))
    rs_q.end(1)
    pl.semaphore_wait(credits.at[4], 1)
    rs_q.to_mate()
    rs_q.end(0)
    get_go.wait()
    late = AllSum(net, "f", vec, vseq, vdp, vmate)
    vec[...] = jnp.zeros_like(vec)

    def norm_back(first, scatter=rs_in, start=0):
        at = pl.ds(pl.multiple_of(start + first, 32), 32)
        xhat, rstd = norm_stats(vt[at, :].astype(F32))
        grad, go = scatter.total(first, 32), kt[at, :].astype(F32)
        vec[:, :D] += jnp.sum(grad * xhat, 0, keepdims=True)
        vec[:, D:] += jnp.sum(grad, 0, keepdims=True)
        g = grad * gain_in[...].astype(F32)
        mean_g = jnp.mean(g, -1, keepdims=True)
        mean_gx = jnp.mean(g * xhat, -1, keepdims=True)
        ot[at, :] = go + (g - mean_g - xhat * mean_gx) * rstd

    pieces(32, 32, lambda first: norm_back(first, rs_pair, 96))
    rs_in.last()
    pieces(96, 32, norm_back)
    late.start()
    local.start(ot, ginp_ref)
    receive_weights(net, "xo", wrecv_o)
    local.start(wrecv_o, wo_ref)
    net.drain("xo")
    rs_u.last()
    turn_weights(rs_u, wsend)
    send_weights(net, "xu", CF, wsend, wrecv_u)
    late.second()
    receive_weights(net, "xu", wrecv_u)
    local.start(wrecv_u, wu_ref)
    net.drain("xu")
    rs_q.last()
    turn_weights(rs_q, wsend)
    late.third()
    send_weights(net, "xq", 3 * CQ, wsend, wrecv_q)
    for d in range(1, 8):
        net.recv(("c", d), bseq.at[lax.rem(net.seq + 8 - d, 8)])
    bias_ref[...] = bseq[...]
    sums_ref[...] = late.done()
    receive_weights(net, "xq", wrecv_q)
    local.start(wrecv_q, wq_ref)
    net.drain()
    local.finish()


def any_spec():
    return pl.BlockSpec(memory_space=pl.ANY)


def vmem_spec():
    return pl.BlockSpec(memory_space=pltpu.VMEM)


def struct(shape, dtype):
    return jax.ShapeDtypeStruct(shape, dtype)


def block_call(x, go, qkv, up, att, down, seg, valid, vectors, qkv_b):
    rates = np.tile(10000.0 ** (-2.0 * np.arange(16, dtype=np.float32) / ROT), 8)[None].astype(np.float32)
    scratch = [
        ((T, D), BF), ((T, D), BF), ((4, 256, D), BF), ((D, 3 * CQ), BF), ((D, CF), BF), ((D, CO), BF), ((2, T, 128), F32),
        ((T, 128), F32), ((NQ, 1, 2 * QB), F32), ((NQ, 2 * QB, CQ), BF), ((T, CQ), BF), ((T, CQ), BF), ((CQ, T), BF),
        ((CQ, T), BF), ((T, CI), BF), ((CI, T), BF), ((4, 2, CF, 256), BF), ((CQ, T), F32), ((NQ, 2 * QB, CQ), BF),
        ((T, CQ), F32), ((T, CQ), F32), ((NQ, 1, 2 * QB), F32), ((NQ, 1, 2 * QB), F32),
        ((1, 2 * QB), F32), ((1, 2 * QB), F32), ((CQ, 2 * QB), F32), ((1, CI), F32),
        ((2, 2, 128, D), BF), ((2, 2, 64, D), BF), ((128, D), BF), ((4, 2, CO, 256), BF), ((2, 2, CO, 256), BF),
        ((2, 2, CO // 2, 256), BF), ((CO, 256), BF),
        ((256, CO), BF), ((8, 32, CO), BF), ((8, 32, CF), BF), ((8, 32, 3 * CQ), BF),
        ((1, CS), F32), ((8, 1, CS), F32), ((8, 1, CS), F32), ((1, 2 * D), F32), ((8, 1, 2 * D), F32),
        ((8, 1, 2 * D), F32), ((1, 2 * D), F32),
    ]
    outs = [
        ((T, D), BF), ((128, D), BF), ((128, D), F32), ((1, 2 * D), F32), ((8, 1, CS), F32), ((8, 32, CO), BF),
        ((8, 32, CF), BF), ((8, 32, 3 * CQ), BF),
    ]
    return pl.pallas_call(
        block_kernel,
        out_shape=[struct(*o) for o in outs],
        in_specs=[any_spec()] * 6 + [vmem_spec()] * 5,
        out_specs=[any_spec()] * 3 + [vmem_spec()] * 2 + [any_spec()] * 3,
        scratch_shapes=[pltpu.VMEM(*s) for s in scratch]
        + [pltpu.SemaphoreType.DMA((SLOTS,)), pltpu.SemaphoreType.DMA((SLOTS,)), pltpu.SemaphoreType.DMA((24,))]
        + [pltpu.SemaphoreType.REGULAR((7,))],
        compiler_params=pltpu.CompilerParams(
            collective_id=1, has_side_effects=True, vmem_limit_bytes=VMEM_LIMIT
        ),
        name="block",
    )(x, go, qkv, up, att, down, seg, valid, vectors, qkv_b, jnp.asarray(rates))


def finish_kernel(
    output_in, ginp_in, sums_in, bias_in, wo_in, wu_in, wq_in,
    output_ref, ginp_ref, ggain_ref, gshift_ref, gqkv_ref, gqkvb_ref, gatt_ref, gup_ref, gupb_ref, gdown_ref, gob_ref,
):
    output_ref[...] = output_in[...]
    ginp_ref[...] = ginp_in[...]
    ggain_ref[...] = sums_in[:, :D]
    gshift_ref[...] = sums_in[:, D:]
    for s in range(8):
        out_part, qkv_part, bias_part = wo_in[s].astype(F32), wq_in[s].astype(F32), bias_in[s]
        gatt_ref[:, s * CQ : (s + 1) * CQ] = out_part[:, :CQ]
        gdown_ref[:, s * CF : (s + 1) * CF] = out_part[:, CQ:]
        gup_ref[:, s * CF : (s + 1) * CF] = wu_in[s].astype(F32)
        gupb_ref[:, s * CF : (s + 1) * CF] = bias_part[:, 3 * CQ : CI]
        gob_ref[:, s * 256 : (s + 1) * 256] = bias_part[:, CI:]
        for j in range(3):
            gqkv_ref[j, :, s * CQ : (s + 1) * CQ] = qkv_part[:, j * CQ : (j + 1) * CQ]
            gqkvb_ref[j : j + 1, s * CQ : (s + 1) * CQ] = bias_part[:, j * CQ : (j + 1) * CQ]


def finish_call(output, ginp, sums, bias, wo, wu, wq):
    outs = [
        ((128, D), BF), ((128, D), F32), ((1, D), F32), ((1, D), F32), ((3, 32, 1024), F32), ((3, 1024), F32),
        ((32, 1024), F32), ((32, 4096), F32), ((1, 4096), F32), ((32, 4096), F32), ((1, D), F32),
    ]
    return pl.pallas_call(
        finish_kernel,
        out_shape=[struct(*o) for o in outs],
        in_specs=[vmem_spec()] * 7,
        out_specs=[vmem_spec()] * 11,
        name="finish",
    )(output, ginp, sums, bias, wo, wu, wq)


def shards(
    inputs, segment_ids, valid_mask, norm_gain, norm_bias, qkv_weight, qkv_bias, attn_out_weight, up_weight, up_bias,
    down_weight, out_bias, grad_out,
):
    parts = block_call(
        inputs[0], grad_out[0], jnp.transpose(qkv_weight, (1, 0, 2)), up_weight, attn_out_weight, down_weight, segment_ids,
        valid_mask, jnp.concatenate([norm_gain, norm_bias, out_bias, up_bias])[None], qkv_bias,
    )
    output, ginp, ggain, gshift, gqkv, gqkvb, gatt, gup, gupb, gdown, gob = finish_call(*parts[1:])
    return (
        output[None], ginp[None], ggain[0], gshift[0], jnp.transpose(gqkv, (1, 0, 2)), gqkvb, gatt, gup, gupb[0], gdown, gob[0],
    )


def solution(mesh):
    placed = (
        P("dp", ("seq", "branch"), None), P("dp", None), P("dp", None), P(), P(), P(("dp", "seq"), None, "branch"),
        P(None, "branch"), P(("dp", "seq"), "branch"), P(("dp", "seq"), "branch"), P("branch"),
        P(("dp", "seq"), "branch"), P(), P("dp", ("seq", "branch"), None),
    )
    return jax.shard_map(
        shards,
        mesh=mesh,
        in_specs=placed,
        out_specs=(
            P("dp", ("seq", "branch"), None), P("dp", ("seq", "branch"), None), P(), P(),
            P(("dp", "seq"), None, "branch"), P(None, "branch"), P(("dp", "seq"), "branch"), P(("dp", "seq"), "branch"),
            P("branch"), P(("dp", "seq"), "branch"), P(),
        ),
        check_vma=False,
    )
```
